32 devices in a mesh: tile: 8 (over z, y), trc: 4 (over x, core).
Axes of the slice: x: 2, y: 2, z: 4, core: 2. Of those that a mesh axis runs over, the one named last changes fastest.
Arguments:
- tracer: float32 [8, 8, 16, 4096], P('trc', None, None, 'tile'), may hold values from -6 to 6
- met_blocks: bfloat16 [128, 16, 256], P('tile'), may hold values from -6 to 6
- intersection_list: int32 [8, 32], replicated, may hold values from -1 to 127, as said below
- entry_index: int32 [8, 16, 8], P('tile'), may hold values from 0 to 31, as said below
- weight_id: int32 [8, 16, 8], P('tile'), may hold values from 0 to 7
- weight_table: bfloat16 [8, 256, 512], replicated, may hold values from -0.125 to 0.125
Outputs:
- tracer_next: float32 [8, 8, 16, 4096], P('trc', None, None, 'tile')
- met_fields: float32 [2, 8, 16, 4096], P(None, None, None, 'tile')
The draws below stay inside these ranges and needn't reach their ends.
Inputs may be any that keep to these rules, and one draw needn't show every extreme that they name: `intersection_list`: row t holds, for each source tile s in order, 4 slots: distinct ids of blocks owned by s (s * 16 to s * 16 + 15), used slots first, the rest -1. Each row has a source with all 4 slots used, the last source fills all its slots in every row, and each source has all 4 slots used in some row. `entry_index`: each entry names a used slot of its tile's list, and every used slot is named by some entry.
All inputs are finite; a program needn't handle non-finite values.
Results may differ from the reference program's by a relative error of at most 0.0003.
Values may be sent and summed in bfloat16 or wider, within the bound.
A program may use at most 64 MiB of HBM per device.

```python
import jax
import jax.numpy as jnp
from jax import lax

LEV = 8
PX = 512
PY = 16
BC = 256
NB_DEV = 16
CAP = 4
K = 8
NW = 8
TILES = 8
NX = 4096
NSPEC = 8
NBLK = 128
FL = 16


def shuffled_prefix(seed_key):
    return jax.random.permutation(seed_key, NB_DEV)[:CAP]


def shuffled_refs(seed_key):
    return jax.random.permutation(seed_key, PY * K)


def intersection_plan(key):
    count_key = jax.random.fold_in(key, 101)
    full_key = jax.random.fold_in(key, 102)
    perm_key = jax.random.fold_in(key, 103)
    pick_key = jax.random.fold_in(key, 104)
    order_key = jax.random.fold_in(key, 105)
    counts = jax.random.randint(count_key, (TILES, TILES), 0, CAP + 1)
    full_source = jax.random.permutation(full_key, TILES)
    source_number = jnp.arange(TILES)[None, :]
    counts = jnp.where(source_number == full_source[:, None], CAP, counts)
    counts = jnp.where(source_number == TILES - 1, CAP, counts)
    local_ids = jax.vmap(shuffled_prefix)(jax.random.split(perm_key, TILES * TILES)).reshape(TILES, TILES, CAP)
    block_ids = jnp.arange(TILES)[None, :, None] * NB_DEV + local_ids
    slot_number = jnp.arange(CAP)
    lists = jnp.where(slot_number[None, None, :] < counts[:, :, None], block_ids, -1).reshape(TILES, TILES * CAP)
    present = lists >= 0
    used_total = jnp.sum(present.astype(jnp.int32), axis=1)
    list_pos = jnp.arange(TILES * CAP)
    order = jnp.argsort(jnp.where(present, list_pos[None, :], TILES * CAP + list_pos[None, :]), axis=1)
    ref_count = PY * K
    picks = jax.random.randint(pick_key, (TILES, ref_count), 0, used_total[:, None])
    ref_pos = jnp.arange(ref_count)
    chosen = jnp.where(ref_pos[None, :] < used_total[:, None], ref_pos[None, :], picks)
    entries = jnp.take_along_axis(order, chosen, axis=1)
    mixing = jax.vmap(shuffled_refs)(jax.random.split(order_key, TILES))
    entries = jnp.take_along_axis(entries, mixing, axis=1).reshape(TILES, PY, K)
    return (lists.astype(jnp.int32), entries.astype(jnp.int32))


def draw_intersection_list(key, part):
    return intersection_plan(key)[0]


def draw_entry_index(key, part):
    return intersection_plan(key)[1]


def plant(array, rng, smallest, top_value):
    longest = array.shape.index(max(array.shape))
    spots = []
    for shift in (0, 1):
        where = [jax.random.randint(jax.random.fold_in(rng, axis), (), 0, length) for axis, length in enumerate(array.shape)]
        where[longest] = (where[longest] + shift) % array.shape[longest]
        spots.append(tuple(where))
    return array.at[spots[0]].set(smallest).at[spots[1]].set(top_value)


def levels(key, dims, shards, smallest, top_value):
    def one(dim, parts):
        heights = jax.random.uniform(jax.random.fold_in(jax.random.fold_in(key, 6), dim), (parts,), jnp.float32, smallest / len(shards), top_value / len(shards))
        return jnp.repeat(jnp.exp(heights), dims[dim] // parts).reshape((-1,) + (1,) * (len(dims) - dim - 1))

    loudness = one(*shards[0])
    for cut in shards[1:]:
        loudness = loudness * one(*cut)
    return loudness


def centred(key, extent, scale, limit, pieces=(), kind=jnp.bfloat16):
    values = jax.random.normal(key, extent, jnp.float32) * scale
    if len(pieces) > 0:
        values = levels(key, extent, pieces, -0.22, 0.18) * values
    return jnp.clip(values, min=-limit, max=limit).astype(kind)


def setup_inputs(seed: int = 0) -> dict:
    arg_keys = jax.random.split(jax.random.key(seed), 7)
    return {
        "tracer": centred(arg_keys[0], (NSPEC, LEV, PY, NX), 1.0, 6.0, ((0, 4), (3, 8)), jnp.float32),
        "met_blocks": centred(arg_keys[1], (NBLK, FL, BC), 1.0, 6.0, ((0, 8),)),
        "intersection_list": draw_intersection_list(jax.random.fold_in(arg_keys[6], 71), 0),
        "entry_index": draw_entry_index(jax.random.fold_in(arg_keys[6], 71), 0),
        "weight_id": plant(jax.random.randint(arg_keys[4], (TILES, PY, K), 0, NW), jax.random.fold_in(arg_keys[4], 1), 0, NW - 1).astype(jnp.int32),
        "weight_table": centred(arg_keys[5], (NW, BC, PX), (K * BC) ** -0.5, 0.125),
    }


def ppm_substep(tracer_ext, courant, massflux):
    face_values = (7.0 / 12.0) * (tracer_ext[..., 1:-2] + tracer_ext[..., 2:-1]) - (1.0 / 12.0) * (tracer_ext[..., :-3] + tracer_ext[..., 3:])
    left_edge = face_values[..., :-1]
    right_edge = face_values[..., 1:]
    centers = tracer_ext[..., 2:-2]
    slopes = right_edge - left_edge
    curvature = 6.0 * centers - 3.0 * (left_edge + right_edge)
    face_courant = courant[..., 3:-2]
    face_mass = massflux[..., 3:-2]
    upwind_abs = jnp.abs(face_courant)
    shape_factor = 1.0 - upwind_abs * (2.0 / 3.0)
    from_left = right_edge[..., :-1] - 0.5 * upwind_abs * (slopes[..., :-1] - shape_factor * curvature[..., :-1])
    from_right = left_edge[..., 1:] + 0.5 * upwind_abs * (slopes[..., 1:] + shape_factor * curvature[..., 1:])
    crossing = jnp.where(face_courant > 0, from_left, from_right)
    fluxes = face_courant * face_mass * crossing
    return tracer_ext[..., 3:-3] - (fluxes[..., 1:] - fluxes[..., :-1])


def periodic(field, width):
    return jnp.concatenate([field[..., -width:], field, field[..., :width]], axis=-1)


def reference(tracer, met_blocks, intersection_list, entry_index, weight_id, weight_table):
    def one_tile(tile_number):
        block_ids = intersection_list[tile_number]
        gathered = jnp.take(met_blocks, jnp.maximum(block_ids, 0), axis=0)
        gathered = jnp.where((block_ids >= 0)[:, None, None], gathered, jnp.zeros((), met_blocks.dtype))
        accumulated = jnp.zeros((PY, FL, PX), jnp.float32)
        for position in range(K):
            sources = jnp.take(gathered, entry_index[tile_number, :, position], axis=0).astype(jnp.float32)
            blocks = jnp.take(weight_table, weight_id[tile_number, :, position], axis=0).astype(jnp.float32)
            accumulated = accumulated + jnp.einsum("jfb,jbd->jfd", sources, blocks)
        return accumulated

    stacked_rows = lax.map(one_tile, jnp.arange(TILES, dtype=jnp.int32))
    raw_fields = jnp.transpose(stacked_rows, (2, 1, 0, 3)).reshape(2, LEV, PY, NX)
    courant = 0.5 * jnp.tanh(raw_fields[0])
    massflux = 1.0 + 0.5 * jnp.tanh(raw_fields[1])
    wide_courant = periodic(courant, 3)
    wide_mass = periodic(massflux, 3)
    first_pass = ppm_substep(periodic(tracer, 3), wide_courant, wide_mass)
    second_pass = ppm_substep(periodic(first_pass, 3), wide_courant, wide_mass)
    return second_pass, jnp.stack([courant, massflux])
```

```python
import functools

import jax
import jax.numpy as jnp
from jax import lax
from jax.experimental import pallas as pl
from jax.experimental.pallas import tpu as pltpu
from jax.sharding import PartitionSpec as P

MESH = pl.DeviceIdType.MESH
EDGE = 8
LANES = 128


def substep(q, positive, c_here, c_side, c_cell):
    width = q.shape[-1]

    def at(array, offset):
        return pltpu.roll(array, (-offset) % width, axis=1)

    q_left = at(q, -1)
    edge = (7.0 / 12.0) * (q_left + q) - (1.0 / 12.0) * (at(q, -2) + at(q, 1))
    side = jnp.where(positive, at(edge, -1), at(edge, 1))
    cell = jnp.where(positive, q_left, q)
    flux = c_here * edge + c_side * side + c_cell * cell
    return q - (at(flux, 1) - flux)


def kernel(
    tiles, cap,
    tracer_hbm, met_hbm, list_hbm, entry_hbm, weight_id_hbm, table_hbm,
    next_ref, fields_ref,
    tracer, blocks, lists, entry, kind, table,
    outgoing, arrived, select, raw, turned, halo_q, halo_m,
    load_sem, send_sem, recv_sem, halo_send, halo_recv,
):
    me = lax.axis_index("tile")
    right, left = lax.rem(me + 1, tiles), lax.rem(me + tiles - 1, tiles)
    rows, columns = tracer.shape
    field_rows, cells = blocks.shape[1], blocks.shape[2]
    depth, row_count = entry.shape
    kinds = table.shape[0]
    slots = tiles * cap
    half = rows // 2

    loads = [
        pltpu.make_async_copy(source, target, load_sem.at[i])
        for i, (source, target) in enumerate(
            (
                (list_hbm, lists),
                (met_hbm, blocks),
                (tracer_hbm, tracer),
                (entry_hbm, entry),
                (weight_id_hbm, kind),
                (table_hbm, table),
            )
        )
    ]
    for load in loads:
        load.start()

    barrier = pltpu.get_barrier_semaphore()
    for offset in range(1, tiles):
        pl.semaphore_signal(
            barrier, inc=1, device_id={"tile": lax.rem(me + offset, tiles)}, device_id_type=MESH
        )

    loads[0].wait()
    loads[1].wait()

    def picked(target, slot):
        number = lists[target, me * cap + slot] - me * blocks.shape[0]
        return blocks[jnp.clip(number, 0, blocks.shape[0] - 1)]

    order = sorted(range(1, tiles), key=lambda o: -min(o, tiles - o))
    for offset in order:
        target = lax.rem(me + offset, tiles)
        for slot in range(cap):
            outgoing[offset, slot] = picked(target, slot)

    pl.semaphore_wait(barrier, tiles - 1)
    sends = []
    for offset in order:
        send = pltpu.make_async_remote_copy(
            src_ref=outgoing.at[offset],
            dst_ref=arrived.at[me],
            send_sem=send_sem.at[offset],
            recv_sem=recv_sem.at[offset],
            device_id={"tile": lax.rem(me + offset, tiles)},
            device_id_type=MESH,
        )
        send.start()
        sends.append(send)
    for slot in range(cap):
        arrived[me, slot] = picked(me, slot)

    def exchange(which, halo):
        copies = []
        for i, (span, target) in enumerate(
            ((pl.ds(0, EDGE), left), (pl.ds(LANES - EDGE, EDGE), right))
        ):
            copy = pltpu.make_async_remote_copy(
                src_ref=turned.at[which, span],
                dst_ref=halo.at[span],
                send_sem=halo_send.at[which, i],
                recv_sem=halo_recv.at[which, i],
                device_id={"tile": target},
                device_id_type=MESH,
            )
            copy.start()
            copies.append(copy)
        return copies

    def turn(which, field):
        first = field[:, :LANES].T
        last = field[:, columns - LANES :].T
        turned[which, :EDGE] = first[:EDGE]
        turned[which, LANES - EDGE :] = last[LANES - EDGE :]

    middle = pl.ds(EDGE, LANES - 2 * EDGE)
    halo_q[middle] = jnp.zeros((LANES - 2 * EDGE, rows), jnp.float32)
    halo_m[middle] = jnp.zeros((LANES - 2 * EDGE, rows), jnp.float32)
    loads[2].wait()
    turn(0, tracer)
    sends += exchange(0, halo_q)
    loads[3].wait()
    loads[4].wait()

    key = (kind[...] * slots + entry[...]).T
    width = slots * field_rows
    column = lax.broadcasted_iota(jnp.int32, (row_count, width), 1)
    slot_of = column // field_rows
    field_of = column - slot_of * field_rows
    keys = [jnp.broadcast_to(key[:, k : k + 1], (row_count, width)) for k in range(depth)]
    masks = [
        jnp.where(field_of == f, 1.0, 0.0).astype(jnp.bfloat16) for f in range(field_rows)
    ]
    for w in range(kinds):
        want = slot_of + w * slots
        count = jnp.zeros((row_count, width), jnp.float32)
        for k in range(depth):
            count = count + jnp.where(keys[k] == want, 1.0, 0.0)
        count = count.astype(jnp.bfloat16)
        for f in range(field_rows):
            select[w, pl.ds(f * row_count, row_count), :] = count * masks[f]

    loads[5].wait()
    for send in sends[: tiles - 1]:
        send.wait_recv()

    entries = arrived[...].reshape(width, cells)
    total = jnp.zeros((rows, columns), jnp.float32)
    for w in range(kinds):
        binned = jnp.dot(select[w], entries, preferred_element_type=jnp.float32)
        high = binned.astype(jnp.bfloat16)
        low = (binned - high.astype(jnp.float32)).astype(jnp.bfloat16)
        both = jnp.concatenate([high, low], axis=0)
        product = jnp.dot(both, table[w], preferred_element_type=jnp.float32)
        total = total + (product[:rows] + product[rows:])
    wave = 0.5 * jnp.tanh(total)
    raw[:half] = wave[:half]
    raw[half:] = 1.0 + wave[half:]
    turn(1, raw)
    met_copies = exchange(1, halo_m)
    fields_ref[...] = raw[...]
    for copy in sends[tiles - 1 :]:
        copy.wait_recv()
    q_edges = halo_q[...].T
    for copy in met_copies:
        copy.wait_recv()
    m_edges = halo_m[...].T

    step = 8
    for start in range(0, half, step):
        here = slice(start, start + step)
        there = slice(half + start, half + start + step)
        courant = jnp.concatenate([raw[here], m_edges[here]], axis=1)
        mass = jnp.concatenate([raw[there], m_edges[there]], axis=1)
        size = jnp.abs(courant)
        linear = 0.5 * size
        square = linear * (1.0 - size * (2.0 / 3.0))
        flow = courant * mass
        c_here = flow * (1.0 - linear - 3.0 * square)
        c_side = flow * (linear - 3.0 * square)
        c_cell = flow * (6.0 * square)
        positive = courant > 0
        for span in (here, there):
            q = jnp.concatenate([tracer[span], q_edges[span]], axis=1)
            for _ in range(2):
                q = substep(q, positive, c_here, c_side, c_cell)
            next_ref[span] = q[:, :columns]

    for copy in sends + met_copies:
        copy.wait_send()


def local(tracer, met_blocks, intersection_list, entry_index, weight_id, weight_table):
    tiles = lax.axis_size("tile")
    cap = intersection_list.shape[1] // tiles
    columns = tracer.shape[-1]
    rows = tracer.size // columns
    row_count = entry_index.shape[1]
    field_rows, cells = met_blocks.shape[1:]
    kinds = weight_table.shape[0]
    width = tiles * cap * field_rows
    flat = (rows, columns)
    assert row_count * field_rows == rows
    anywhere = pl.BlockSpec(memory_space=pl.ANY)
    vmem = pl.BlockSpec(memory_space=pltpu.VMEM)
    tracer_next, fields = pl.pallas_call(
        functools.partial(kernel, tiles, cap),
        out_shape=(jax.ShapeDtypeStruct(flat, jnp.float32),) * 2,
        in_specs=[anywhere] * 6,
        out_specs=(vmem, vmem),
        scratch_shapes=[
            pltpu.VMEM(flat, jnp.float32),
            pltpu.VMEM(met_blocks.shape, jnp.bfloat16),
            pltpu.SMEM(intersection_list.shape, jnp.int32),
            pltpu.VMEM(entry_index.shape[:0:-1], jnp.int32),
            pltpu.VMEM(weight_id.shape[:0:-1], jnp.int32),
            pltpu.VMEM(weight_table.shape, jnp.bfloat16),
            pltpu.VMEM((tiles, cap, field_rows, cells), jnp.bfloat16),
            pltpu.VMEM((tiles, cap, field_rows, cells), jnp.bfloat16),
            pltpu.VMEM((kinds, rows, width), jnp.bfloat16),
            pltpu.VMEM(flat, jnp.float32),
            pltpu.VMEM((2, LANES, rows), jnp.float32),
            pltpu.VMEM((LANES, rows), jnp.float32),
            pltpu.VMEM((LANES, rows), jnp.float32),
            pltpu.SemaphoreType.DMA((6,)),
            pltpu.SemaphoreType.DMA((tiles,)),
            pltpu.SemaphoreType.DMA((tiles,)),
            pltpu.SemaphoreType.DMA((2, 2)),
            pltpu.SemaphoreType.DMA((2, 2)),
        ],
        compiler_params=pltpu.CompilerParams(
            collective_id=0, has_side_effects=True, vmem_limit_bytes=60 * 2**20
        ),
        name="regrid_and_advect",
    )(tracer.reshape(flat), met_blocks, intersection_list, entry_index[0].T, weight_id[0].T, weight_table)
    return tracer_next.reshape(tracer.shape), fields.reshape((2,) + tracer.shape[1:])


def solution(mesh):
    return jax.shard_map(
        local,
        mesh=mesh,
        in_specs=(
            P("trc", None, None, "tile"),
            P("tile", None, None),
            P(),
            P("tile", None, None),
            P("tile", None, None),
            P(),
        ),
        out_specs=(P("trc", None, None, "tile"), P(None, None, None, "tile")),
        check_vma=False,
    )
```

```python
import functools

import jax
import jax.numpy as jnp
from jax import lax
from jax.experimental import pallas as pl
from jax.experimental.pallas import tpu as pltpu
from jax.sharding import PartitionSpec as P

MESH = pl.DeviceIdType.MESH
EDGE = 8
LANES = 128


def substep(q, positive, c_here, c_side, c_cell):
    width = q.shape[-1]

    def at(array, offset):
        return pltpu.roll(array, (-offset) % width, axis=array.ndim - 1)

    q_left = at(q, -1)
    edge = (7.0 / 12.0) * (q_left + q) - (1.0 / 12.0) * (at(q, -2) + at(q, 1))
    side = jnp.where(positive, at(edge, -1), at(edge, 1))
    cell = jnp.where(positive, q_left, q)
    flux = c_here * edge + c_side * side + c_cell * cell
    return q - (at(flux, 1) - flux)


STEP = 64


def advect(tracer, raw, q_edges, m_edges, next_hbm, fields_hbm, result, field_sem, store_sem):
    rows, columns = tracer.shape
    half = rows // 2
    fields_copy = pltpu.make_async_copy(raw, fields_hbm, field_sem.at[0])
    fields_copy.start()
    copies = []
    for number, start in enumerate(range(0, half, STEP)):
        here = slice(start, start + STEP)
        there = slice(half + start, half + start + STEP)
        courant = jnp.concatenate([raw[here], m_edges[here]], axis=1)
        mass = jnp.concatenate([raw[there], m_edges[there]], axis=1)
        size = jnp.abs(courant)
        linear = 0.5 * size
        square = linear * (1.0 - size * (2.0 / 3.0))
        flow = courant * mass
        c_here = flow * (1.0 - linear - 3.0 * square)
        c_side = flow * (linear - 3.0 * square)
        c_cell = flow * (6.0 * square)
        positive = courant > 0
        both = [positive, c_here, c_side, c_cell]
        both = [jnp.concatenate([one, one], axis=0) for one in both]
        q = jnp.concatenate(
            [
                jnp.concatenate([tracer[span], q_edges[span]], axis=1)
                for span in (here, there)
            ],
            axis=0,
        )
        for _ in range(2):
            q = substep(q, *both)
        for i, span in enumerate((here, there)):
            result[span] = q[i * STEP : (i + 1) * STEP, :columns]
            rows_done = pl.ds(i * half + start, STEP)
            copy = pltpu.make_async_copy(
                result.at[rows_done], next_hbm.at[rows_done], store_sem.at[number, i]
            )
            copy.start()
            copies.append(copy)
    fields_copy.wait()
    for copy in copies:
        copy.wait()


def kernel(
    tiles, cap,
    tracer_hbm, met_hbm, list_hbm, entry_hbm, weight_id_hbm, table_hbm,
    tracer, raw, q_edges, m_edges,
    blocks, lists, entry, kind, table,
    outgoing, arrived, select, turned, halo_q, halo_m,
    load_sem, send_sem, recv_sem, halo_send, halo_recv,
):
    me = lax.axis_index("tile")
    right, left = lax.rem(me + 1, tiles), lax.rem(me + tiles - 1, tiles)
    rows, columns = tracer.shape
    field_rows, cells = blocks.shape[1], blocks.shape[2]
    depth, row_count = entry.shape
    kinds = table.shape[0]
    slots = tiles * cap
    half = rows // 2

    loads = [
        pltpu.make_async_copy(source, target, load_sem.at[i])
        for i, (source, target) in enumerate(
            (
                (list_hbm, lists),
                (met_hbm, blocks),
                (tracer_hbm, tracer),
                (entry_hbm, entry),
                (weight_id_hbm, kind),
                (table_hbm, table),
            )
        )
    ]
    for load in loads:
        load.start()

    barrier = pltpu.get_barrier_semaphore()
    for offset in range(1, tiles):
        pl.semaphore_signal(
            barrier, inc=1, device_id={"tile": lax.rem(me + offset, tiles)}, device_id_type=MESH
        )

    loads[0].wait()
    loads[1].wait()

    def picked(target, slot):
        number = lists[target, me * cap + slot] - me * blocks.shape[0]
        return blocks[jnp.clip(number, 0, blocks.shape[0] - 1)]

    order = sorted(range(1, tiles), key=lambda o: -min(o, tiles - o))
    for offset in order:
        target = lax.rem(me + offset, tiles)
        for slot in range(cap):
            outgoing[offset, slot] = picked(target, slot)

    pl.semaphore_wait(barrier, tiles - 1)
    sends = []
    for offset in order:
        send = pltpu.make_async_remote_copy(
            src_ref=outgoing.at[offset],
            dst_ref=arrived.at[me],
            send_sem=send_sem.at[offset],
            recv_sem=recv_sem.at[offset],
            device_id={"tile": lax.rem(me + offset, tiles)},
            device_id_type=MESH,
        )
        send.start()
        sends.append(send)
    for slot in range(cap):
        arrived[me, slot] = picked(me, slot)

    def exchange(which, halo):
        copies = []
        for i, (span, target) in enumerate(
            ((pl.ds(0, EDGE), left), (pl.ds(LANES - EDGE, EDGE), right))
        ):
            copy = pltpu.make_async_remote_copy(
                src_ref=turned.at[which, span],
                dst_ref=halo.at[span],
                send_sem=halo_send.at[which, i],
                recv_sem=halo_recv.at[which, i],
                device_id={"tile": target},
                device_id_type=MESH,
            )
            copy.start()
            copies.append(copy)
        return copies

    def turn(which, field):
        first = field[:, :LANES].T
        last = field[:, columns - LANES :].T
        turned[which, :EDGE] = first[:EDGE]
        turned[which, LANES - EDGE :] = last[LANES - EDGE :]

    middle = pl.ds(EDGE, LANES - 2 * EDGE)
    halo_q[middle] = jnp.zeros((LANES - 2 * EDGE, rows), jnp.float32)
    halo_m[middle] = jnp.zeros((LANES - 2 * EDGE, rows), jnp.float32)
    loads[2].wait()
    turn(0, tracer)
    sends += exchange(0, halo_q)
    loads[3].wait()
    loads[4].wait()

    key = (kind[...] * slots + entry[...]).T
    width = slots * field_rows
    column = lax.broadcasted_iota(jnp.int32, (row_count, width), 1)
    slot_of = column // field_rows
    field_of = column - slot_of * field_rows
    keys = [jnp.broadcast_to(key[:, k : k + 1], (row_count, width)) for k in range(depth)]
    masks = [
        jnp.where(field_of == f, 1.0, 0.0).astype(jnp.bfloat16) for f in range(field_rows)
    ]
    for w in range(kinds):
        want = slot_of + w * slots
        count = jnp.zeros((row_count, width), jnp.float32)
        for k in range(depth):
            count = count + jnp.where(keys[k] == want, 1.0, 0.0)
        count = count.astype(jnp.bfloat16)
        for f in range(field_rows):
            select[w, pl.ds(f * row_count, row_count), :] = count * masks[f]

    loads[5].wait()
    for send in sends[: tiles - 1]:
        send.wait_recv()

    entries = arrived[...].reshape(width, cells)
    total = jnp.zeros((rows, columns), jnp.float32)
    for w in range(kinds):
        binned = jnp.dot(select[w], entries, preferred_element_type=jnp.float32)
        high = binned.astype(jnp.bfloat16)
        low = (binned - high.astype(jnp.float32)).astype(jnp.bfloat16)
        both = jnp.concatenate([high, low], axis=0)
        product = jnp.dot(both, table[w], preferred_element_type=jnp.float32)
        total = total + (product[:rows] + product[rows:])
    wave = 0.5 * jnp.tanh(total)
    raw[:half] = wave[:half]
    raw[half:] = 1.0 + wave[half:]
    turn(1, raw)
    met_copies = exchange(1, halo_m)
    for copy in sends[tiles - 1 :]:
        copy.wait_recv()
    q_edges[...] = halo_q[...].T
    for copy in met_copies:
        copy.wait_recv()
    m_edges[...] = halo_m[...].T

    for copy in sends + met_copies:
        copy.wait_send()


def local(tracer, met_blocks, intersection_list, entry_index, weight_id, weight_table):
    tiles = lax.axis_size("tile")
    cap = intersection_list.shape[1] // tiles
    columns = tracer.shape[-1]
    rows = tracer.size // columns
    row_count = entry_index.shape[1]
    field_rows, cells = met_blocks.shape[1:]
    kinds = weight_table.shape[0]
    width = tiles * cap * field_rows
    flat = (rows, columns)
    assert row_count * field_rows == rows
    hbm = pl.BlockSpec(memory_space=pltpu.HBM)
    vmem = pl.BlockSpec(memory_space=pltpu.VMEM)
    edges = (rows, LANES)
    held = pl.pallas_call(
        functools.partial(kernel, tiles, cap),
        out_shape=tuple(jax.ShapeDtypeStruct(one, jnp.float32) for one in (flat, flat, edges, edges)),
        in_specs=[hbm] * 6,
        out_specs=(vmem,) * 4,
        scratch_shapes=[
            pltpu.VMEM(met_blocks.shape, jnp.bfloat16),
            pltpu.SMEM(intersection_list.shape, jnp.int32),
            pltpu.VMEM(entry_index.shape[:0:-1], jnp.int32),
            pltpu.VMEM(weight_id.shape[:0:-1], jnp.int32),
            pltpu.VMEM(weight_table.shape, jnp.bfloat16),
            pltpu.VMEM((tiles, cap, field_rows, cells), jnp.bfloat16),
            pltpu.VMEM((tiles, cap, field_rows, cells), jnp.bfloat16),
            pltpu.VMEM((kinds, rows, width), jnp.bfloat16),
            pltpu.VMEM((2, LANES, rows), jnp.float32),
            pltpu.VMEM((LANES, rows), jnp.float32),
            pltpu.VMEM((LANES, rows), jnp.float32),
            pltpu.SemaphoreType.DMA((6,)),
            pltpu.SemaphoreType.DMA((tiles,)),
            pltpu.SemaphoreType.DMA((tiles,)),
            pltpu.SemaphoreType.DMA((2, 2)),
            pltpu.SemaphoreType.DMA((2, 2)),
        ],
        compiler_params=pltpu.CompilerParams(
            collective_id=0, has_side_effects=True, vmem_limit_bytes=40 * 2**20
        ),
        name="gather_and_regrid",
    )(
        *(
            pltpu.with_memory_space_constraint(one, pltpu.HBM)
            for one in (
                tracer.reshape(flat),
                met_blocks,
                intersection_list,
                entry_index[0].T,
                weight_id[0].T,
                weight_table,
            )
        )
    )
    tracer_next, fields = pl.pallas_call(
        advect,
        out_shape=(jax.ShapeDtypeStruct(flat, jnp.float32),) * 2,
        in_specs=[vmem] * 4,
        out_specs=(hbm, hbm),
        scratch_shapes=[
            pltpu.VMEM(flat, jnp.float32),
            pltpu.SemaphoreType.DMA((1,)),
            pltpu.SemaphoreType.DMA((rows // 2 // STEP, 2)),
        ],
        compiler_params=pltpu.CompilerParams(vmem_limit_bytes=40 * 2**20),
        name="advect",
    )(*held)
    return tracer_next.reshape(tracer.shape), fields.reshape((2,) + tracer.shape[1:])


def solution(mesh):
    return jax.shard_map(
        local,
        mesh=mesh,
        in_specs=(
            P("trc", None, None, "tile"),
            P("tile", None, None),
            P(),
            P("tile", None, None),
            P("tile", None, None),
            P(),
        ),
        out_specs=(P("trc", None, None, "tile"), P(None, None, None, "tile")),
        check_vma=False,
    )
```

```python
import functools
import math

import jax
import jax.numpy as jnp
from jax import lax
from jax.experimental import pallas as pl
from jax.experimental.pallas import tpu as pltpu
from jax.sharding import PartitionSpec as P

MESH = pl.DeviceIdType.MESH
EDGE = 8
GROUP = 2
BATCHES = 2
LANES = 128


def substep(q, positive, c_here, c_side, c_cell):
    width = q.shape[-1]

    def at(array, offset):
        return pltpu.roll(array, (-offset) % width, axis=array.ndim - 1)

    q_left = at(q, -1)
    edge = (7.0 / 12.0) * (q_left + q) - (1.0 / 12.0) * (at(q, -2) + at(q, 1))
    side = jnp.where(positive, at(edge, -1), at(edge, 1))
    cell = jnp.where(positive, q_left, q)
    flux = c_here * edge + c_side * side + c_cell * cell
    return q - (at(flux, 1) - flux)


STEP = 64


def advect(tracer, raw, q_edges, m_edges, next_hbm, fields_hbm, result, field_sem, store_sem):
    rows, columns = tracer.shape
    half = rows // 2
    fields_copy = pltpu.make_async_copy(raw, fields_hbm, field_sem.at[0])
    fields_copy.start()
    copies = []
    for number, start in enumerate(range(0, half, STEP)):
        here = slice(start, start + STEP)
        there = slice(half + start, half + start + STEP)
        courant = jnp.concatenate([raw[here], m_edges[here]], axis=1)
        mass = jnp.concatenate([raw[there], m_edges[there]], axis=1)
        size = jnp.abs(courant)
        linear = 0.5 * size
        square = linear * (1.0 - size * (2.0 / 3.0))
        flow = courant * mass
        c_here = flow * (1.0 - linear - 3.0 * square)
        c_side = flow * (linear - 3.0 * square)
        c_cell = flow * (6.0 * square)
        positive = courant > 0
        both = [positive, c_here, c_side, c_cell]
        both = [jnp.concatenate([one, one], axis=0) for one in both]
        q = jnp.concatenate(
            [
                jnp.concatenate([tracer[span], q_edges[span]], axis=1)
                for span in (here, there)
            ],
            axis=0,
        )
        for _ in range(2):
            q = substep(q, *both)
        for i, span in enumerate((here, there)):
            result[span] = q[i * STEP : (i + 1) * STEP, :columns]
            rows_done = pl.ds(i * half + start, STEP)
            copy = pltpu.make_async_copy(
                result.at[rows_done], next_hbm.at[rows_done], store_sem.at[number, i]
            )
            copy.start()
            copies.append(copy)
    fields_copy.wait()
    for copy in copies:
        copy.wait()


def kernel(
    tiles, cap, group, batches,
    tracer_hbm, met_hbm, list_hbm, entry_hbm, weight_id_hbm, table_hbm,
    tracer, raw, q_edges, m_edges,
    blocks, lists, entry, kind, outer, inner,
    outgoing, arrived, select, binned, turned, halo_q, halo_m,
    load_sem, send_sem, recv_sem, pass_send, pass_recv, halo_send, halo_recv,
):
    me = lax.axis_index("tile")
    trc = lax.axis_index("trc")
    member = lax.rem(trc, group)
    right, left = lax.rem(me + 1, tiles), lax.rem(me + tiles - 1, tiles)
    rows, columns = tracer.shape
    field_rows, cells = blocks.shape[1], blocks.shape[2]
    depth, row_count = entry.shape
    kinds = table_hbm.shape[0] // cells
    slots = tiles * cap
    share = cap // group
    half = rows // 2

    loads = [
        pltpu.make_async_copy(source, target, load_sem.at[i])
        for i, (source, target) in enumerate(
            (
                (list_hbm, lists),
                (met_hbm, blocks),
                (tracer_hbm, tracer),
                (entry_hbm, entry),
                (weight_id_hbm, kind),
                (table_hbm.at[:, pl.ds(0, LANES)], outer.at[:, pl.ds(0, LANES)]),
                (table_hbm.at[:, pl.ds(columns - LANES, LANES)], outer.at[:, pl.ds(LANES, LANES)]),
                (table_hbm.at[:, pl.ds(LANES, columns - 2 * LANES)], inner),
            )
        )
    ]
    for load in loads:
        load.start()

    def across(bit):
        return trc + bit - 2 * bit * lax.rem(member // bit, 2)

    bits = [bit for bit in (2, 1) if bit < group]

    barrier = pltpu.get_barrier_semaphore()
    for offset in range(1, tiles):
        pl.semaphore_signal(
            barrier, inc=1, device_id={"tile": lax.rem(me + offset, tiles)}, device_id_type=MESH
        )
    for bit in bits:
        pl.semaphore_signal(barrier, inc=1, device_id={"trc": across(bit)}, device_id_type=MESH)

    loads[0].wait()
    loads[1].wait()

    def picked(target, slot):
        number = lists[target, me * cap + slot] - me * blocks.shape[0]
        return blocks[jnp.clip(number, 0, blocks.shape[0] - 1)]

    order = sorted(range(1, tiles), key=lambda o: -min(o, tiles - o))
    for offset in order:
        target = lax.rem(me + offset, tiles)
        for slot in range(share):
            outgoing[offset, slot] = picked(target, member * share + slot)

    pl.semaphore_wait(barrier, tiles - 1 + len(bits))
    sends = {}
    for offset in order:
        send = pltpu.make_async_remote_copy(
            src_ref=outgoing.at[offset],
            dst_ref=arrived.at[member, offset],
            send_sem=send_sem.at[offset],
            recv_sem=recv_sem.at[offset],
            device_id={"tile": lax.rem(me + offset, tiles)},
            device_id_type=MESH,
        )
        send.start()
        sends[offset] = send
    for slot in range(cap):
        arrived[slot // share, 0, slot % share] = picked(me, slot)

    def exchange(which, halo):
        copies = []
        for i, (span, target) in enumerate(
            ((pl.ds(0, EDGE), left), (pl.ds(LANES - EDGE, EDGE), right))
        ):
            copy = pltpu.make_async_remote_copy(
                src_ref=turned.at[which, span],
                dst_ref=halo.at[span],
                send_sem=halo_send.at[which, i],
                recv_sem=halo_recv.at[which, i],
                device_id={"tile": target},
                device_id_type=MESH,
            )
            copy.start()
            copies.append(copy)
        return copies

    def turn(which, first, last):
        turned[which, :EDGE] = first.T[:EDGE]
        turned[which, LANES - EDGE :] = last.T[LANES - EDGE :]

    middle = pl.ds(EDGE, LANES - 2 * EDGE)
    halo_q[middle] = jnp.zeros((LANES - 2 * EDGE, rows), jnp.float32)
    halo_m[middle] = jnp.zeros((LANES - 2 * EDGE, rows), jnp.float32)
    loads[2].wait()
    turn(0, tracer[:, :LANES], tracer[:, columns - LANES :])
    q_copies = exchange(0, halo_q)
    loads[3].wait()
    loads[4].wait()

    key = (kind[...] * slots + entry[...]).T
    width = slots * field_rows
    column = lax.broadcasted_iota(jnp.int32, (row_count, width), 1)
    place = column // field_rows
    field_of = column - place * field_rows
    member_of = place // (tiles * share)
    offset_of = place // share - member_of * tiles
    source_of = me - offset_of
    source_of = jnp.where(source_of < 0, source_of + tiles, source_of)
    within = place - (place // share) * share
    slot_of = source_of * cap + member_of * share + within
    keys = [jnp.broadcast_to(key[:, k : k + 1], (row_count, width)) for k in range(depth)]
    masks = [
        jnp.where(field_of == f, 1.0, 0.0).astype(jnp.bfloat16) for f in range(field_rows)
    ]
    for w in range(kinds):
        want = slot_of + w * slots
        count = jnp.zeros((row_count, width), jnp.float32)
        for k in range(depth):
            count = count + jnp.where(keys[k] == want, 1.0, 0.0)
        count = count.astype(jnp.bfloat16)
        for f in range(field_rows):
            select[w, pl.ds(f * row_count, row_count), :] = count * masks[f]

    def forward(which, i, bit, region):
        first, count = batches[i]
        span = arrived.at[region, pl.ds(first, count)]
        copy = pltpu.make_async_remote_copy(
            src_ref=span,
            dst_ref=span,
            send_sem=pass_send.at[i, which],
            recv_sem=pass_recv.at[i, which],
            device_id={"trc": across(bit)},
            device_id_type=MESH,
        )
        copy.start()
        passed.append(copy)
        return copy

    passed, late, crossed = [], [], []
    for i, (first, count) in enumerate(batches):
        for offset in range(first, first + count):
            sends[offset].wait_recv()
        if group == 4:
            crossed.append(forward(2, i, 2, member))
        if group > 1:
            late.append(forward(0, i, 1, member))
    if group == 4:
        for i in range(len(batches)):
            crossed[i].wait_recv()
            late.append(forward(1, i, 1, across(2) - trc + member))
    for copy in late:
        copy.wait_recv()

    entries = arrived[...].reshape(width, cells)
    for w in range(kinds):
        part = jnp.dot(select[w], entries, preferred_element_type=jnp.float32)
        high = part.astype(jnp.bfloat16)
        low = (part - high.astype(jnp.float32)).astype(jnp.bfloat16)
        binned[pl.ds(0, rows), pl.ds(w * cells, cells)] = high
        binned[pl.ds(rows, rows), pl.ds(w * cells, cells)] = low

    def fields(table):
        product = jnp.dot(binned[...], table[...], preferred_element_type=jnp.float32)
        wave = 0.5 * jnp.tanh(product[:rows] + product[rows:])
        return jnp.concatenate([wave[:half], 1.0 + wave[half:]], axis=0)

    loads[5].wait()
    loads[6].wait()
    ends = fields(outer)
    turn(1, ends[:, :LANES], ends[:, LANES:])
    m_copies = exchange(1, halo_m)
    raw[:, :LANES] = ends[:, :LANES]
    raw[:, columns - LANES :] = ends[:, LANES:]
    loads[7].wait()
    raw[:, LANES : columns - LANES] = fields(inner)
    for copy in q_copies:
        copy.wait_recv()
    q_edges[...] = halo_q[...].T
    for copy in m_copies:
        copy.wait_recv()
    m_edges[...] = halo_m[...].T

    for copy in [*sends.values(), *passed, *q_copies, *m_copies]:
        copy.wait_send()


def local(tracer, met_blocks, intersection_list, entry_index, weight_id, weight_table):
    tiles = lax.axis_size("tile")
    cap = intersection_list.shape[1] // tiles
    group = math.gcd(math.gcd(cap, lax.axis_size("trc")), GROUP)
    cuts = [1 + (tiles - 1) * i // BATCHES for i in range(BATCHES + 1)]
    batches = [(low, high - low) for low, high in zip(cuts, cuts[1:])]
    columns = tracer.shape[-1]
    rows = tracer.size // columns
    row_count = entry_index.shape[1]
    field_rows, cells = met_blocks.shape[1:]
    kinds = weight_table.shape[0]
    width = tiles * cap * field_rows
    flat = (rows, columns)
    assert row_count * field_rows == rows
    hbm = pl.BlockSpec(memory_space=pltpu.HBM)
    vmem = pl.BlockSpec(memory_space=pltpu.VMEM)
    edges = (rows, LANES)
    held = pl.pallas_call(
        functools.partial(kernel, tiles, cap, group, batches),
        out_shape=tuple(jax.ShapeDtypeStruct(one, jnp.float32) for one in (flat, flat, edges, edges)),
        in_specs=[hbm] * 6,
        out_specs=(vmem,) * 4,
        scratch_shapes=[
            pltpu.VMEM(met_blocks.shape, jnp.bfloat16),
            pltpu.SMEM(intersection_list.shape, jnp.int32),
            pltpu.VMEM(entry_index.shape[:0:-1], jnp.int32),
            pltpu.VMEM(weight_id.shape[:0:-1], jnp.int32),
            pltpu.VMEM((kinds * cells, 2 * LANES), jnp.bfloat16),
            pltpu.VMEM((kinds * cells, columns - 2 * LANES), jnp.bfloat16),
            pltpu.VMEM((tiles, cap // group, field_rows, cells), jnp.bfloat16),
            pltpu.VMEM((group, tiles, cap // group, field_rows, cells), jnp.bfloat16),
            pltpu.VMEM((kinds, rows, width), jnp.bfloat16),
            pltpu.VMEM((2 * rows, kinds * cells), jnp.bfloat16),
            pltpu.VMEM((2, LANES, rows), jnp.float32),
            pltpu.VMEM((LANES, rows), jnp.float32),
            pltpu.VMEM((LANES, rows), jnp.float32),
            pltpu.SemaphoreType.DMA((8,)),
            pltpu.SemaphoreType.DMA((tiles,)),
            pltpu.SemaphoreType.DMA((tiles,)),
            pltpu.SemaphoreType.DMA((len(batches), 3)),
            pltpu.SemaphoreType.DMA((len(batches), 3)),
            pltpu.SemaphoreType.DMA((2, 2)),
            pltpu.SemaphoreType.DMA((2, 2)),
        ],
        compiler_params=pltpu.CompilerParams(
            collective_id=0, has_side_effects=True, vmem_limit_bytes=40 * 2**20
        ),
        name="gather_and_regrid",
    )(
        *(
            pltpu.with_memory_space_constraint(one, pltpu.HBM)
            for one in (
                tracer.reshape(flat),
                met_blocks,
                intersection_list,
                entry_index[0].T,
                weight_id[0].T,
                weight_table.reshape(kinds * cells, columns),
            )
        )
    )
    tracer_next, fields = pl.pallas_call(
        advect,
        out_shape=(jax.ShapeDtypeStruct(flat, jnp.float32),) * 2,
        in_specs=[vmem] * 4,
        out_specs=(hbm, hbm),
        scratch_shapes=[
            pltpu.VMEM(flat, jnp.float32),
            pltpu.SemaphoreType.DMA((1,)),
            pltpu.SemaphoreType.DMA((rows // 2 // STEP, 2)),
        ],
        compiler_params=pltpu.CompilerParams(vmem_limit_bytes=40 * 2**20),
        name="advect",
    )(*held)
    return tracer_next.reshape(tracer.shape), fields.reshape((2,) + tracer.shape[1:])


def solution(mesh):
    return jax.shard_map(
        local,
        mesh=mesh,
        in_specs=(
            P("trc", None, None, "tile"),
            P("tile", None, None),
            P(),
            P("tile", None, None),
            P("tile", None, None),
            P(),
        ),
        out_specs=(P("trc", None, None, "tile"), P(None, None, None, "tile")),
        check_vma=False,
    )
```

```python
import functools
import math

import jax
import jax.numpy as jnp
from jax import lax
from jax.experimental import pallas as pl
from jax.experimental.pallas import tpu as pltpu
from jax.sharding import PartitionSpec as P

MESH = pl.DeviceIdType.MESH
EDGE = 8
GROUP = 2
BATCHES = 2
LANES = 128


def coefficients(courant, mass):
    size = jnp.abs(courant)
    linear = 0.5 * size
    square = linear * (1.0 - size * (2.0 / 3.0))
    flow = courant * mass
    return (
        courant > 0,
        flow * (1.0 - linear - 3.0 * square),
        flow * (linear - 3.0 * square),
        flow * (6.0 * square),
    )


def advance(q, positive, c_here, c_side, c_cell, axis):
    width = q.shape[axis]

    def at(array, offset):
        return pltpu.roll(array, (-offset) % width, axis=axis)

    for _ in range(2):
        q_left = at(q, -1)
        edge = (7.0 / 12.0) * (q_left + q) - (1.0 / 12.0) * (at(q, -2) + at(q, 1))
        side = jnp.where(positive, at(edge, -1), at(edge, 1))
        cell = jnp.where(positive, q_left, q)
        flux = c_here * edge + c_side * side + c_cell * cell
        q = q - (at(flux, 1) - flux)
    return q


STEP = 64


def write(done, raw, next_hbm, fields_hbm, sems):
    copies = [
        pltpu.make_async_copy(done, next_hbm, sems.at[0]),
        pltpu.make_async_copy(raw, fields_hbm, sems.at[1]),
    ]
    for copy in copies:
        copy.start()
    for copy in copies:
        copy.wait()


def kernel(
    tiles, cap, group, batches,
    tracer_hbm, met_hbm, list_hbm, entry_hbm, weight_id_hbm, table_hbm,
    done, raw,
    tracer, blocks, lists, entry, kind, outer, inner,
    outgoing, arrived, select, binned, turned, halo_q, halo_m,
    load_sem, send_sem, recv_sem, pass_send, pass_recv, halo_send, halo_recv,
):
    me = lax.axis_index("tile")
    trc = lax.axis_index("trc")
    member = lax.rem(trc, group)
    right, left = lax.rem(me + 1, tiles), lax.rem(me + tiles - 1, tiles)
    rows, columns = tracer.shape
    field_rows, cells = blocks.shape[1], blocks.shape[2]
    depth, row_count = entry.shape
    kinds = table_hbm.shape[0] // cells
    slots = tiles * cap
    share = cap // group
    half = rows // 2

    loads = [
        pltpu.make_async_copy(source, target, load_sem.at[i])
        for i, (source, target) in enumerate(
            (
                (list_hbm, lists),
                (met_hbm, blocks),
                (tracer_hbm, tracer),
                (entry_hbm, entry),
                (weight_id_hbm, kind),
                (table_hbm.at[:, pl.ds(0, LANES)], outer.at[:, pl.ds(0, LANES)]),
                (table_hbm.at[:, pl.ds(columns - LANES, LANES)], outer.at[:, pl.ds(LANES, LANES)]),
                (table_hbm.at[:, pl.ds(LANES, columns - 2 * LANES)], inner),
            )
        )
    ]
    for load in loads:
        load.start()

    def across(bit):
        return trc + bit - 2 * bit * lax.rem(member // bit, 2)

    bits = [bit for bit in (2, 1) if bit < group]

    barrier = pltpu.get_barrier_semaphore()
    for offset in range(1, tiles):
        pl.semaphore_signal(
            barrier, inc=1, device_id={"tile": lax.rem(me + offset, tiles)}, device_id_type=MESH
        )
    for bit in bits:
        pl.semaphore_signal(barrier, inc=1, device_id={"trc": across(bit)}, device_id_type=MESH)

    loads[0].wait()
    loads[1].wait()

    def picked(target, slot):
        number = lists[target, me * cap + slot] - me * blocks.shape[0]
        return blocks[jnp.clip(number, 0, blocks.shape[0] - 1)]

    order = sorted(range(1, tiles), key=lambda o: -min(o, tiles - o))
    for offset in order:
        target = lax.rem(me + offset, tiles)
        for slot in range(share):
            outgoing[offset, slot] = picked(target, member * share + slot)

    pl.semaphore_wait(barrier, tiles - 1 + len(bits))
    sends = {}
    for offset in order:
        send = pltpu.make_async_remote_copy(
            src_ref=outgoing.at[offset],
            dst_ref=arrived.at[member, offset],
            send_sem=send_sem.at[offset],
            recv_sem=recv_sem.at[offset],
            device_id={"tile": lax.rem(me + offset, tiles)},
            device_id_type=MESH,
        )
        send.start()
        sends[offset] = send
    for slot in range(cap):
        arrived[slot // share, 0, slot % share] = picked(me, slot)

    def exchange(which, halo):
        copies = []
        for i, (span, target) in enumerate(
            ((pl.ds(0, EDGE), left), (pl.ds(LANES - EDGE, EDGE), right))
        ):
            copy = pltpu.make_async_remote_copy(
                src_ref=turned.at[which, span],
                dst_ref=halo.at[span],
                send_sem=halo_send.at[which, i],
                recv_sem=halo_recv.at[which, i],
                device_id={"tile": target},
                device_id_type=MESH,
            )
            copy.start()
            copies.append(copy)
        return copies

    def turn(which, first, last):
        turned[which, : 2 * EDGE] = first.T[: 2 * EDGE]
        turned[which, LANES - 2 * EDGE :] = last.T[LANES - 2 * EDGE :]

    loads[2].wait()
    turn(0, tracer[:, :LANES], tracer[:, columns - LANES :])
    q_copies = exchange(0, halo_q)
    loads[3].wait()
    loads[4].wait()

    key = (kind[...] * slots + entry[...]).T
    width = slots * field_rows
    column = lax.broadcasted_iota(jnp.int32, (row_count, width), 1)
    place = column // field_rows
    field_of = column - place * field_rows
    member_of = place // (tiles * share)
    offset_of = place // share - member_of * tiles
    source_of = me - offset_of
    source_of = jnp.where(source_of < 0, source_of + tiles, source_of)
    within = place - (place // share) * share
    slot_of = source_of * cap + member_of * share + within
    keys = [jnp.broadcast_to(key[:, k : k + 1], (row_count, width)) for k in range(depth)]
    masks = [
        jnp.where(field_of == f, 1.0, 0.0).astype(jnp.bfloat16) for f in range(field_rows)
    ]
    for w in range(kinds):
        want = slot_of + w * slots
        count = jnp.zeros((row_count, width), jnp.float32)
        for k in range(depth):
            count = count + jnp.where(keys[k] == want, 1.0, 0.0)
        count = count.astype(jnp.bfloat16)
        for f in range(field_rows):
            select[w, pl.ds(f * row_count, row_count), :] = count * masks[f]

    def forward(which, i, bit, region):
        first, count = batches[i]
        span = arrived.at[region, pl.ds(first, count)]
        copy = pltpu.make_async_remote_copy(
            src_ref=span,
            dst_ref=span,
            send_sem=pass_send.at[i, which],
            recv_sem=pass_recv.at[i, which],
            device_id={"trc": across(bit)},
            device_id_type=MESH,
        )
        copy.start()
        passed.append(copy)
        return copy

    passed, late, crossed = [], [], []
    for i, (first, count) in enumerate(batches):
        for offset in range(first, first + count):
            sends[offset].wait_recv()
        if group == 4:
            crossed.append(forward(2, i, 2, member))
        if group > 1:
            late.append(forward(0, i, 1, member))
    if group == 4:
        for i in range(len(batches)):
            crossed[i].wait_recv()
            late.append(forward(1, i, 1, across(2) - trc + member))
    for copy in late:
        copy.wait_recv()

    entries = arrived[...].reshape(width, cells)
    for w in range(kinds):
        part = jnp.dot(select[w], entries, preferred_element_type=jnp.float32)
        high = part.astype(jnp.bfloat16)
        low = (part - high.astype(jnp.float32)).astype(jnp.bfloat16)
        binned[pl.ds(0, rows), pl.ds(w * cells, cells)] = high
        binned[pl.ds(rows, rows), pl.ds(w * cells, cells)] = low

    def fields(table):
        product = jnp.dot(binned[...], table[...], preferred_element_type=jnp.float32)
        wave = 0.5 * jnp.tanh(product[:rows] + product[rows:])
        return jnp.concatenate([wave[:half], 1.0 + wave[half:]], axis=0)

    loads[5].wait()
    loads[6].wait()
    ends = fields(outer)
    turn(1, ends[:, :LANES], ends[:, LANES:])
    m_copies = exchange(1, halo_m)
    raw[:, :LANES] = ends[:, :LANES]
    raw[:, columns - LANES :] = ends[:, LANES:]
    loads[7].wait()
    raw[:, LANES : columns - LANES] = fields(inner)

    for start in range(0, half, STEP):
        here = slice(start, start + STEP)
        there = slice(half + start, half + start + STEP)
        factors = [
            jnp.concatenate([one, one], axis=0) for one in coefficients(raw[here], raw[there])
        ]
        q = advance(jnp.concatenate([tracer[here], tracer[there]], axis=0), *factors, 1)
        done[here] = q[:STEP]
        done[there] = q[STEP:]

    for copy in [*q_copies, *m_copies]:
        copy.wait_recv()

    def stripe(q_stripe, m_stripe):
        factors = [
            jnp.concatenate([one, one], axis=1)
            for one in coefficients(m_stripe[:, :half], m_stripe[:, half:])
        ]
        return advance(q_stripe, *factors, 0)[EDGE : 2 * EDGE]

    first, last = stripe(
        *(
            jnp.concatenate([halo[LANES - EDGE :], turned[which, : 2 * EDGE]], axis=0)
            for which, halo in enumerate((halo_q, halo_m))
        )
    ), stripe(
        *(
            jnp.concatenate([turned[which, LANES - 2 * EDGE :], halo[:EDGE]], axis=0)
            for which, halo in enumerate((halo_q, halo_m))
        )
    )
    gap = jnp.zeros((LANES - 2 * EDGE, rows), jnp.float32)
    fixed = jnp.concatenate([first, gap, last], axis=0).T
    lane = lax.broadcasted_iota(jnp.int32, (rows, LANES), 1)
    done[:, :LANES] = jnp.where(lane < EDGE, fixed, done[:, :LANES])
    tail = slice(columns - LANES, columns)
    done[:, tail] = jnp.where(lane >= LANES - EDGE, fixed, done[:, tail])

    for copy in [*sends.values(), *passed, *q_copies, *m_copies]:
        copy.wait_send()


def local(tracer, met_blocks, intersection_list, entry_index, weight_id, weight_table):
    tiles = lax.axis_size("tile")
    cap = intersection_list.shape[1] // tiles
    group = math.gcd(math.gcd(cap, lax.axis_size("trc")), GROUP)
    cuts = [1 + (tiles - 1) * i // BATCHES for i in range(BATCHES + 1)]
    batches = [(low, high - low) for low, high in zip(cuts, cuts[1:])]
    columns = tracer.shape[-1]
    rows = tracer.size // columns
    row_count = entry_index.shape[1]
    field_rows, cells = met_blocks.shape[1:]
    kinds = weight_table.shape[0]
    width = tiles * cap * field_rows
    flat = (rows, columns)
    assert row_count * field_rows == rows
    hbm = pl.BlockSpec(memory_space=pltpu.HBM)
    vmem = pl.BlockSpec(memory_space=pltpu.VMEM)
    held = pl.pallas_call(
        functools.partial(kernel, tiles, cap, group, batches),
        out_shape=tuple(jax.ShapeDtypeStruct(one, jnp.float32) for one in (flat, flat)),
        in_specs=[hbm] * 6,
        out_specs=(vmem,) * 2,
        scratch_shapes=[
            pltpu.VMEM(flat, jnp.float32),
            pltpu.VMEM(met_blocks.shape, jnp.bfloat16),
            pltpu.SMEM(intersection_list.shape, jnp.int32),
            pltpu.VMEM(entry_index.shape[:0:-1], jnp.int32),
            pltpu.VMEM(weight_id.shape[:0:-1], jnp.int32),
            pltpu.VMEM((kinds * cells, 2 * LANES), jnp.bfloat16),
            pltpu.VMEM((kinds * cells, columns - 2 * LANES), jnp.bfloat16),
            pltpu.VMEM((tiles, cap // group, field_rows, cells), jnp.bfloat16),
            pltpu.VMEM((group, tiles, cap // group, field_rows, cells), jnp.bfloat16),
            pltpu.VMEM((kinds, rows, width), jnp.bfloat16),
            pltpu.VMEM((2 * rows, kinds * cells), jnp.bfloat16),
            pltpu.VMEM((2, LANES, rows), jnp.float32),
            pltpu.VMEM((LANES, rows), jnp.float32),
            pltpu.VMEM((LANES, rows), jnp.float32),
            pltpu.SemaphoreType.DMA((8,)),
            pltpu.SemaphoreType.DMA((tiles,)),
            pltpu.SemaphoreType.DMA((tiles,)),
            pltpu.SemaphoreType.DMA((len(batches), 3)),
            pltpu.SemaphoreType.DMA((len(batches), 3)),
            pltpu.SemaphoreType.DMA((2, 2)),
            pltpu.SemaphoreType.DMA((2, 2)),
        ],
        compiler_params=pltpu.CompilerParams(
            collective_id=0, has_side_effects=True, vmem_limit_bytes=40 * 2**20
        ),
        name="gather_and_regrid",
    )(
        *(
            pltpu.with_memory_space_constraint(one, pltpu.HBM)
            for one in (
                tracer.reshape(flat),
                met_blocks,
                intersection_list,
                entry_index[0].T,
                weight_id[0].T,
                weight_table.reshape(kinds * cells, columns),
            )
        )
    )
    tracer_next, fields = pl.pallas_call(
        write,
        out_shape=(jax.ShapeDtypeStruct(flat, jnp.float32),) * 2,
        in_specs=[vmem] * 2,
        out_specs=(hbm, hbm),
        scratch_shapes=[pltpu.SemaphoreType.DMA((2,))],
        compiler_params=pltpu.CompilerParams(vmem_limit_bytes=16 * 2**20),
        name="write",
    )(*held)
    return tracer_next.reshape(tracer.shape), fields.reshape((2,) + tracer.shape[1:])


def solution(mesh):
    return jax.shard_map(
        local,
        mesh=mesh,
        in_specs=(
            P("trc", None, None, "tile"),
            P("tile", None, None),
            P(),
            P("tile", None, None),
            P("tile", None, None),
            P(),
        ),
        out_specs=(P("trc", None, None, "tile"), P(None, None, None, "tile")),
        check_vma=False,
    )
```

```python
import functools
import math

import jax
import jax.numpy as jnp
from jax import lax
from jax.experimental import pallas as pl
from jax.experimental.pallas import tpu as pltpu
from jax.sharding import PartitionSpec as P

MESH = pl.DeviceIdType.MESH
EDGE = 8
GROUP = 2
BATCHES = 2
LANES = 128


def coefficients(courant, mass):
    size = jnp.abs(courant)
    linear = 0.5 * size
    square = linear * (1.0 - size * (2.0 / 3.0))
    flow = courant * mass
    return (
        courant > 0,
        flow * (1.0 - linear - 3.0 * square),
        flow * (linear - 3.0 * square),
        flow * (6.0 * square),
    )


def advance(q, positive, c_here, c_side, c_cell, axis):
    width = q.shape[axis]

    def at(array, offset):
        return pltpu.roll(array, (-offset) % width, axis=axis)

    for _ in range(2):
        q_left = at(q, -1)
        edge = (7.0 / 12.0) * (q_left + q) - (1.0 / 12.0) * (at(q, -2) + at(q, 1))
        side = jnp.where(positive, at(edge, -1), at(edge, 1))
        cell = jnp.where(positive, q_left, q)
        flux = c_here * edge + c_side * side + c_cell * cell
        q = q - (at(flux, 1) - flux)
    return q


STEP = 64


def write(done, raw, next_hbm, fields_hbm, sems):
    copies = [
        pltpu.make_async_copy(done, next_hbm, sems.at[0]),
        pltpu.make_async_copy(raw, fields_hbm, sems.at[1]),
    ]
    for copy in copies:
        copy.start()
    for copy in copies:
        copy.wait()


def kernel(
    tiles, cap, group, batches,
    tracer_hbm, met_hbm, list_hbm, entry_hbm, weight_id_hbm, table_hbm,
    done, raw,
    tracer, blocks, lists, entry, kind, outer, inner,
    outgoing, arrived, select, binned, turned, halo_q, halo_m,
    load_sem, send_sem, recv_sem, pass_send, pass_recv, halo_send, halo_recv,
):
    me = lax.axis_index("tile")
    trc = lax.axis_index("trc")
    member = lax.rem(trc, group)
    right, left = lax.rem(me + 1, tiles), lax.rem(me + tiles - 1, tiles)
    rows, columns = tracer.shape
    field_rows, cells = blocks.shape[1], blocks.shape[2]
    depth, row_count = entry.shape
    kinds = table_hbm.shape[0] // cells
    slots = tiles * cap
    share = cap // group
    half = rows // 2

    loads = [
        pltpu.make_async_copy(source, target, load_sem.at[i])
        for i, (source, target) in enumerate(
            (
                (list_hbm, lists),
                (met_hbm, blocks),
                (tracer_hbm, tracer),
                (entry_hbm, entry),
                (weight_id_hbm, kind),
                (table_hbm.at[:, pl.ds(0, LANES)], outer.at[:, pl.ds(0, LANES)]),
                (table_hbm.at[:, pl.ds(columns - LANES, LANES)], outer.at[:, pl.ds(LANES, LANES)]),
                (table_hbm.at[:, pl.ds(LANES, columns - 2 * LANES)], inner),
            )
        )
    ]
    def across(bit):
        return trc + bit - 2 * bit * lax.rem(member // bit, 2)

    bits = [bit for bit in (2, 1) if bit < group]

    barrier = pltpu.get_barrier_semaphore()
    for offset in range(1, tiles):
        pl.semaphore_signal(
            barrier, inc=1, device_id={"tile": lax.rem(me + offset, tiles)}, device_id_type=MESH
        )
    for bit in bits:
        pl.semaphore_signal(barrier, inc=1, device_id={"trc": across(bit)}, device_id_type=MESH)

    for load in loads:
        load.start()

    loads[0].wait()
    loads[1].wait()

    def picked(target, slot):
        number = lists[target, me * cap + slot] - me * blocks.shape[0]
        return blocks[jnp.clip(number, 0, blocks.shape[0] - 1)]

    order = sorted(range(1, tiles), key=lambda o: min(o, tiles - o))
    for offset in order:
        target = lax.rem(me + offset, tiles)
        for slot in range(share):
            outgoing[offset, slot] = picked(target, member * share + slot)

    pl.semaphore_wait(barrier, tiles - 1 + len(bits))
    sends = {}
    for offset in order:
        send = pltpu.make_async_remote_copy(
            src_ref=outgoing.at[offset],
            dst_ref=arrived.at[member, offset],
            send_sem=send_sem.at[offset],
            recv_sem=recv_sem.at[offset],
            device_id={"tile": lax.rem(me + offset, tiles)},
            device_id_type=MESH,
        )
        send.start()
        sends[offset] = send
    for slot in range(cap):
        arrived[slot // share, 0, slot % share] = picked(me, slot)

    def exchange(which, halo):
        copies = []
        for i, (span, target) in enumerate(
            ((pl.ds(0, EDGE), left), (pl.ds(LANES - EDGE, EDGE), right))
        ):
            copy = pltpu.make_async_remote_copy(
                src_ref=turned.at[which, span],
                dst_ref=halo.at[span],
                send_sem=halo_send.at[which, i],
                recv_sem=halo_recv.at[which, i],
                device_id={"tile": target},
                device_id_type=MESH,
            )
            copy.start()
            copies.append(copy)
        return copies

    def turn(which, first, last):
        turned[which, : 2 * EDGE] = first.T[: 2 * EDGE]
        turned[which, LANES - 2 * EDGE :] = last.T[LANES - 2 * EDGE :]

    loads[3].wait()
    loads[4].wait()

    key = (kind[...] * slots + entry[...]).T
    width = slots * field_rows
    column = lax.broadcasted_iota(jnp.int32, (row_count, width), 1)
    place = column // field_rows
    field_of = column - place * field_rows
    member_of = place // (tiles * share)
    offset_of = place // share - member_of * tiles
    source_of = me - offset_of
    source_of = jnp.where(source_of < 0, source_of + tiles, source_of)
    within = place - (place // share) * share
    slot_of = source_of * cap + member_of * share + within
    keys = [jnp.broadcast_to(key[:, k : k + 1], (row_count, width)) for k in range(depth)]
    masks = [
        jnp.where(field_of == f, 1.0, 0.0).astype(jnp.bfloat16) for f in range(field_rows)
    ]
    for w in range(kinds):
        want = slot_of + w * slots
        count = jnp.zeros((row_count, width), jnp.float32)
        for k in range(depth):
            count = count + jnp.where(keys[k] == want, 1.0, 0.0)
        count = count.astype(jnp.bfloat16)
        for f in range(field_rows):
            select[w, pl.ds(f * row_count, row_count), :] = count * masks[f]

    def forward(which, i, bit, region):
        first, count = batches[i]
        span = arrived.at[region, pl.ds(first, count)]
        copy = pltpu.make_async_remote_copy(
            src_ref=span,
            dst_ref=span,
            send_sem=pass_send.at[i, which],
            recv_sem=pass_recv.at[i, which],
            device_id={"trc": across(bit)},
            device_id_type=MESH,
        )
        copy.start()
        passed.append(copy)
        return copy

    passed, late, crossed = [], [], []
    for i, (first, count) in enumerate(batches):
        for offset in range(first, first + count):
            sends[offset].wait_recv()
        if group == 4:
            crossed.append(forward(2, i, 2, member))
        if group > 1:
            late.append(forward(0, i, 1, member))
    if group == 4:
        for i in range(len(batches)):
            crossed[i].wait_recv()
            late.append(forward(1, i, 1, across(2) - trc + member))
    loads[2].wait()
    turn(0, tracer[:, :LANES], tracer[:, columns - LANES :])
    q_copies = exchange(0, halo_q)
    for copy in late:
        copy.wait_recv()

    entries = arrived[...].reshape(width, cells)
    for w in range(kinds):
        part = jnp.dot(select[w], entries, preferred_element_type=jnp.float32)
        high = part.astype(jnp.bfloat16)
        low = (part - high.astype(jnp.float32)).astype(jnp.bfloat16)
        binned[pl.ds(0, rows), pl.ds(w * cells, cells)] = high
        binned[pl.ds(rows, rows), pl.ds(w * cells, cells)] = low

    def fields(table):
        product = jnp.dot(binned[...], table[...], preferred_element_type=jnp.float32)
        wave = 0.5 * jnp.tanh(product[:rows] + product[rows:])
        return jnp.concatenate([wave[:half], 1.0 + wave[half:]], axis=0)

    loads[5].wait()
    loads[6].wait()
    ends = fields(outer)
    turn(1, ends[:, :LANES], ends[:, LANES:])
    m_copies = exchange(1, halo_m)
    raw[:, :LANES] = ends[:, :LANES]
    raw[:, columns - LANES :] = ends[:, LANES:]
    loads[7].wait()
    raw[:, LANES : columns - LANES] = fields(inner)

    for start in range(0, half, STEP):
        here = slice(start, start + STEP)
        there = slice(half + start, half + start + STEP)
        factors = [
            jnp.concatenate([one, one], axis=0) for one in coefficients(raw[here], raw[there])
        ]
        q = advance(jnp.concatenate([tracer[here], tracer[there]], axis=0), *factors, 1)
        done[here] = q[:STEP]
        done[there] = q[STEP:]

    for copy in [*q_copies, *m_copies]:
        copy.wait_recv()

    def stripe(q_stripe, m_stripe):
        factors = [
            jnp.concatenate([one, one], axis=1)
            for one in coefficients(m_stripe[:, :half], m_stripe[:, half:])
        ]
        return advance(q_stripe, *factors, 0)[EDGE : 2 * EDGE]

    first, last = stripe(
        *(
            jnp.concatenate([halo[LANES - EDGE :], turned[which, : 2 * EDGE]], axis=0)
            for which, halo in enumerate((halo_q, halo_m))
        )
    ), stripe(
        *(
            jnp.concatenate([turned[which, LANES - 2 * EDGE :], halo[:EDGE]], axis=0)
            for which, halo in enumerate((halo_q, halo_m))
        )
    )
    gap = jnp.zeros((LANES - 2 * EDGE, rows), jnp.float32)
    fixed = jnp.concatenate([first, gap, last], axis=0).T
    lane = lax.broadcasted_iota(jnp.int32, (rows, LANES), 1)
    done[:, :LANES] = jnp.where(lane < EDGE, fixed, done[:, :LANES])
    tail = slice(columns - LANES, columns)
    done[:, tail] = jnp.where(lane >= LANES - EDGE, fixed, done[:, tail])

    for copy in [*sends.values(), *passed, *q_copies, *m_copies]:
        copy.wait_send()


def local(tracer, met_blocks, intersection_list, entry_index, weight_id, weight_table):
    tiles = lax.axis_size("tile")
    cap = intersection_list.shape[1] // tiles
    group = math.gcd(math.gcd(cap, lax.axis_size("trc")), GROUP)
    cuts = [1 + (tiles - 1) * i // BATCHES for i in range(BATCHES + 1)]
    batches = [(low, high - low) for low, high in zip(cuts, cuts[1:])]
    columns = tracer.shape[-1]
    rows = tracer.size // columns
    row_count = entry_index.shape[1]
    field_rows, cells = met_blocks.shape[1:]
    kinds = weight_table.shape[0]
    width = tiles * cap * field_rows
    flat = (rows, columns)
    assert row_count * field_rows == rows
    hbm = pl.BlockSpec(memory_space=pltpu.HBM)
    vmem = pl.BlockSpec(memory_space=pltpu.VMEM)
    held = pl.pallas_call(
        functools.partial(kernel, tiles, cap, group, batches),
        out_shape=tuple(jax.ShapeDtypeStruct(one, jnp.float32) for one in (flat, flat)),
        in_specs=[hbm] * 6,
        out_specs=(vmem,) * 2,
        scratch_shapes=[
            pltpu.VMEM(flat, jnp.float32),
            pltpu.VMEM(met_blocks.shape, jnp.bfloat16),
            pltpu.SMEM(intersection_list.shape, jnp.int32),
            pltpu.VMEM(entry_index.shape[:0:-1], jnp.int32),
            pltpu.VMEM(weight_id.shape[:0:-1], jnp.int32),
            pltpu.VMEM((kinds * cells, 2 * LANES), jnp.bfloat16),
            pltpu.VMEM((kinds * cells, columns - 2 * LANES), jnp.bfloat16),
            pltpu.VMEM((tiles, cap // group, field_rows, cells), jnp.bfloat16),
            pltpu.VMEM((group, tiles, cap // group, field_rows, cells), jnp.bfloat16),
            pltpu.VMEM((kinds, rows, width), jnp.bfloat16),
            pltpu.VMEM((2 * rows, kinds * cells), jnp.bfloat16),
            pltpu.VMEM((2, LANES, rows), jnp.float32),
            pltpu.VMEM((LANES, rows), jnp.float32),
            pltpu.VMEM((LANES, rows), jnp.float32),
            pltpu.SemaphoreType.DMA((8,)),
            pltpu.SemaphoreType.DMA((tiles,)),
            pltpu.SemaphoreType.DMA((tiles,)),
            pltpu.SemaphoreType.DMA((len(batches), 3)),
            pltpu.SemaphoreType.DMA((len(batches), 3)),
            pltpu.SemaphoreType.DMA((2, 2)),
            pltpu.SemaphoreType.DMA((2, 2)),
        ],
        compiler_params=pltpu.CompilerParams(
            collective_id=0, has_side_effects=True, vmem_limit_bytes=40 * 2**20
        ),
        name="gather_and_regrid",
    )(
        *(
            pltpu.with_memory_space_constraint(one, pltpu.HBM)
            for one in (
                tracer.reshape(flat),
                met_blocks,
                intersection_list,
                entry_index[0].T,
                weight_id[0].T,
                weight_table.reshape(kinds * cells, columns),
            )
        )
    )
    tracer_next, fields = pl.pallas_call(
        write,
        out_shape=(jax.ShapeDtypeStruct(flat, jnp.float32),) * 2,
        in_specs=[vmem] * 2,
        out_specs=(hbm, hbm),
        scratch_shapes=[pltpu.SemaphoreType.DMA((2,))],
        compiler_params=pltpu.CompilerParams(vmem_limit_bytes=16 * 2**20),
        name="write",
    )(*held)
    return tracer_next.reshape(tracer.shape), fields.reshape((2,) + tracer.shape[1:])


def solution(mesh):
    return jax.shard_map(
        local,
        mesh=mesh,
        in_specs=(
            P("trc", None, None, "tile"),
            P("tile", None, None),
            P(),
            P("tile", None, None),
            P("tile", None, None),
            P(),
        ),
        out_specs=(P("trc", None, None, "tile"), P(None, None, None, "tile")),
        check_vma=False,
    )
```
